128 devices in a mesh: tm: 16 (over y, z), rows: 8 (over x, core).
Axes of the slice: x: 4, y: 4, z: 4, core: 2. Of those that a mesh axis runs over, the one named last changes fastest.
Arguments:
- video: bfloat16 [128, 64, 128, 128], P('tm', 'rows'), may hold values from -6 to 6
- w_space: bfloat16 [3, 3, 128, 128], replicated, may hold values from -0.1875 to 0.1875
- w_time: bfloat16 [3, 128, 128], replicated, may hold values from -0.3125 to 0.3125
- w_pixel: bfloat16 [3, 128], replicated, may hold values from -0.5 to 0.5
- w_patch: bfloat16 [192, 256], replicated, may hold values from -0.4375 to 0.4375
- w_logit: bfloat16 [256], replicated, may hold values from -0.375 to 0.375
- grad_out: bfloat16 [128, 64, 128, 128], P('tm', 'rows'), may hold values from -6 to 6
Outputs:
- input_grad: bfloat16 [128, 64, 128, 128], P('tm', 'rows')
- space_grad: float32 [3, 3, 128, 128], replicated
- time_grad: float32 [3, 128, 128], replicated
- logits: float32 [128, 8, 16], P(('tm', 'rows'))
The draws below stay inside these ranges and needn't reach their ends.
All inputs are finite; a program needn't handle non-finite values.
Results may differ from the reference program's by a relative error of at most 0.008.
Values may be sent and summed in bfloat16 or wider, within the bound.
A program may use at most 128 MiB of HBM per device.

```python
import math
import jax
import jax.numpy as jnp
from jax import lax

C = 128
DH = 256
PATCH = 8
W = 128
F = 128
H = 64


def block_levels(stream_key, shape, pieces, least, high):
    factor_of = 1.0
    for axis_at, parts in pieces:
        heights = jax.random.uniform(jax.random.fold_in(jax.random.fold_in(stream_key, 6), axis_at), (parts,), jnp.float32, least / len(pieces), high / len(pieces))
        factor_of = factor_of * jnp.repeat(jnp.exp(heights), shape[axis_at] // parts).reshape((-1,) + (1,) * (len(shape) - 1 - axis_at))
    return factor_of


def normal_values(stream_key, dims, scale, reach, pieces=(), held_as=jnp.bfloat16):
    entries = scale * jax.random.normal(stream_key, dims, jnp.float32)
    if pieces:
        entries = entries * block_levels(stream_key, dims, pieces, -0.22, 0.18)
    return jnp.clip(entries, -reach, reach).astype(held_as)


def setup_inputs(seed: int = 0) -> dict:
    seeds = jax.random.split(jax.random.key(seed), 8)
    return {
        "video": normal_values(seeds[0], (F, H, W, C), 1.0, 6.0, ((0, 16), (1, 8))),
        "w_space": normal_values(seeds[1], (3, 3, C, C), (9 * C) ** -0.5, 0.1875),
        "w_time": normal_values(seeds[2], (3, C, C), (3 * C) ** -0.5, 0.3125),
        "w_pixel": normal_values(seeds[3], (3, C), C ** -0.5, 0.5),
        "w_patch": normal_values(seeds[4], (3 * PATCH * PATCH, DH), (3 * PATCH * PATCH) ** -0.5, 0.4375),
        "w_logit": normal_values(seeds[5], (DH,), DH ** -0.5, 0.375),
        "grad_out": normal_values(seeds[6], (F, H, W, C), 1.0, 6.0, ((0, 16), (1, 8))),
    }


def space_conv(frame, w_space):
    height, width, chans = frame.shape
    padded = jnp.pad(frame, ((1, 1), (1, 1), (0, 0)))
    total = jnp.zeros((height * width, chans), jnp.float32)
    for row_off in range(3):
        for col_off in range(3):
            window = padded[row_off:row_off + height, col_off:col_off + width].reshape(-1, chans)
            total = total + jnp.dot(window, w_space[row_off, col_off], preferred_element_type=jnp.float32)
    return total.reshape(height, width, chans)

def judge(pixels, w_patch, w_logit):
    values = pixels.astype(jnp.float32)
    center = lax.optimization_barrier(jnp.mean(values, axis=(1, 2, 3), keepdims=True))
    spread = lax.optimization_barrier(jnp.mean((values - center) * (values - center), axis=(1, 2, 3), keepdims=True))
    normed = ((values - center) * lax.rsqrt(spread + 1e-05)).astype(jnp.bfloat16)
    count, height, colours, width = normed.shape
    tiles = normed.reshape(count, height // PATCH, PATCH, colours, width // PATCH, PATCH)
    tiles = tiles.transpose(0, 1, 4, 2, 3, 5).reshape(-1, colours * PATCH * PATCH)
    inner = jax.nn.leaky_relu(jnp.dot(tiles, w_patch, preferred_element_type=jnp.float32), 0.2)
    return jnp.dot(inner, w_logit.astype(jnp.float32)).reshape(count, height // PATCH, width // PATCH)

def reference(video, w_space, w_time, w_pixel, w_patch, w_logit, grad_out):
    chans = C
    pre_act = lax.map(lambda frame: space_conv(frame, w_space), video)
    hidden = jax.nn.silu(pre_act).astype(jnp.bfloat16)
    history = jnp.concatenate([jnp.zeros((2, H, W, chans), jnp.bfloat16), hidden], axis=0)
    temporal = jnp.zeros((F * H * W, chans), jnp.float32)
    for lag in range(3):
        temporal = temporal + jnp.dot(history[2 - lag:2 - lag + F].reshape(-1, chans), w_time[lag], preferred_element_type=jnp.float32)
    block = (video.reshape(-1, chans).astype(jnp.float32) + temporal).astype(jnp.bfloat16).reshape(F, H, W, chans)
    pixels = jnp.einsum('fhwc,kc->fhkw', block.astype(jnp.float32), w_pixel.astype(jnp.float32)).astype(jnp.bfloat16)
    logits = judge(pixels, w_patch, w_logit)
    factor = 1.0 / math.sqrt(F * H * W)
    flat_grad = grad_out.reshape(-1, chans)
    time_parts = []
    for lag in range(3):
        time_parts.append(jnp.dot(history[2 - lag:2 - lag + F].reshape(-1, chans).T, flat_grad, preferred_element_type=jnp.float32))
    time_grad = jnp.stack(time_parts) * factor
    future = jnp.concatenate([grad_out, jnp.zeros((2, H, W, chans), jnp.bfloat16)], axis=0)
    back_hidden = jnp.zeros((F * H * W, chans), jnp.float32)
    for lag in range(3):
        back_hidden = back_hidden + jnp.dot(future[lag:lag + F].reshape(-1, chans), w_time[lag].T, preferred_element_type=jnp.float32)
    flat_pre = pre_act.reshape(-1, chans)
    sigma = jax.nn.sigmoid(flat_pre)
    back_pre = (back_hidden * sigma * (1.0 + flat_pre * (1.0 - sigma))).astype(jnp.bfloat16)
    video_pad = jnp.pad(video, ((0, 0), (1, 1), (1, 1), (0, 0)))
    space_rows = []
    for row_off in range(3):
        space_cols = []
        for col_off in range(3):
            window = video_pad[:, row_off:row_off + H, col_off:col_off + W].reshape(-1, chans)
            space_cols.append(jnp.dot(window.T, back_pre, preferred_element_type=jnp.float32))
        space_rows.append(jnp.stack(space_cols))
    space_grad = jnp.stack(space_rows) * factor
    back_pad = jnp.pad(back_pre.reshape(F, H, W, chans), ((0, 0), (1, 1), (1, 1), (0, 0)))
    total = flat_grad.astype(jnp.float32)
    for row_off in range(3):
        for col_off in range(3):
            window = back_pad[:, 2 - row_off:2 - row_off + H, 2 - col_off:2 - col_off + W].reshape(-1, chans)
            total = total + jnp.dot(window, w_space[row_off, col_off].T, preferred_element_type=jnp.float32)
    input_grad = total.astype(jnp.bfloat16).reshape(F, H, W, chans)
    return (input_grad, space_grad, time_grad, logits)
```

```python
import functools
import math

import jax
import jax.numpy as jnp
from jax import lax
from jax.experimental import pallas as pl
from jax.experimental.pallas import tpu as pltpu
from jax.sharding import PartitionSpec as P

PATCH = 8
C = 128
MESH = pl.DeviceIdType.MESH
F32 = jnp.float32
BF16 = jnp.bfloat16


def mm(a, b):
    return jnp.dot(a, b, preferred_element_type=F32)


def mm_nt(a, b):
    return lax.dot_general(a, b, (((1,), (1,)), ((), ())), preferred_element_type=F32)


def shifted(cells, col, step):
    size = cells.shape[0]
    moved = pltpu.roll(cells, (size - step) % size, 0)
    return jnp.where(col == (0 if step < 0 else 127), 0.0, moved)


def kernel(
    nt, nr,
    video, w_space, w_time, w_pixel, w_patch, w_logit, grad,
    out_ig, out_ar, out_lg,
    vpad, gpad, hid, bpad, bcat, vtr, bh, og,
    wf, wb, wt, wp, wpf, wv, stage,
    yb, hsend, hrecv, stat, lgs, pix,
    acc, buf1, s1, buf2, buf3, ob,
    lsem, osem,
    vs, vr, gs, gr, bs, br, hs, hr, ss, sr, ls, lr,
    s1s, s1r, s2s, s2r, s3s, s3r, s4s, s4r, s5s, s5r,
):
    t = lax.axis_index("tm")
    r = lax.axis_index("rows")
    core = lax.rem(r, 2)
    xpos = r // 2
    nx = nr // 2
    partner = r + 1 - 2 * core
    fd, rd, width, _ = video.shape

    def remote(src, dst, ssem, rsem, tt, rr):
        return pltpu.make_async_remote_copy(
            src_ref=src, dst_ref=dst, send_sem=ssem, recv_sem=rsem,
            device_id=(tt, rr), device_id_type=MESH,
        )

    barrier = pltpu.get_barrier_semaphore()
    for d in range(1, nr):
        pl.semaphore_signal(barrier, inc=1, device_id=(t, lax.rem(r + d, nr)), device_id_type=MESH)
    for d in range(1, nt):
        pl.semaphore_signal(barrier, inc=1, device_id=(lax.rem(t + d, nt), r), device_id_type=MESH)

    load_v = pltpu.make_async_copy(video, vpad.at[:, 1 : rd + 1], lsem.at[0])
    load_g = pltpu.make_async_copy(grad, gpad.at[0:fd], lsem.at[1])
    load_v.start()
    load_g.start()

    pl.semaphore_wait(barrier, nr - 1 + nt - 1)

    to_up = remote(video.at[:, 0], vpad.at[:, rd + 1], vs.at[0], vr.at[0], t, jnp.maximum(r - 1, 0))
    to_down = remote(video.at[:, rd - 1], vpad.at[:, 0], vs.at[1], vr.at[1], t, jnp.minimum(r + 1, nr - 1))
    to_prev = remote(grad.at[0:2], gpad.at[fd : fd + 2], gs.at[0], gr.at[0], jnp.maximum(t - 1, 0), r)

    @pl.when(r > 0)
    def _():
        to_up.start()

    @pl.when(r < nr - 1)
    def _():
        to_down.start()

    @pl.when(t > 0)
    def _():
        to_prev.start()

    @pl.when(r == 0)
    def _():
        vpad[:, 0] = jnp.zeros((fd, width, C), BF16)
        bpad[:, 0] = jnp.zeros((fd, width, C), BF16)

    @pl.when(r == nr - 1)
    def _():
        vpad[:, rd + 1] = jnp.zeros((fd, width, C), BF16)
        bpad[:, rd + 1] = jnp.zeros((fd, width, C), BF16)

    @pl.when(t == nt - 1)
    def _():
        gpad[fd : fd + 2] = jnp.zeros((2, rd, width, C), BF16)

    @pl.when(t == 0)
    def _():
        hrecv[...] = jnp.zeros((width, C), F32)

    blank = jnp.zeros((C, C), BF16)
    for dj in range(3):
        for a in range(4):
            for o in range(2):
                rows_at = slice(a * C, (a + 1) * C)
                cols_at = slice(o * C, (o + 1) * C)
                wf[dj, rows_at, cols_at] = w_space[a - o, dj] if 0 <= a - o <= 2 else blank
                di = o + 2 - a
                wb[dj, rows_at, cols_at] = w_space[di, dj].T if 0 <= di <= 2 else blank
    for a in range(4):
        for o in range(2):
            wt[a * C : (a + 1) * C, o * C : (o + 1) * C] = (
                w_time[a - o].T if 0 <= a - o <= 2 else blank
            )

    stage[...] = jnp.zeros((4, C, C), F32)
    pixel_rows = w_pixel[...].astype(F32)
    for g in range(4):
        stage[g, 24 * g : 24 * g + 3, :] = pixel_rows
    eye = (
        lax.broadcasted_iota(jnp.int32, (C, C), 0) == lax.broadcasted_iota(jnp.int32, (C, C), 1)
    ).astype(BF16)
    a_video = mm_nt(eye, stage[0].astype(BF16))
    a_hid = mm_nt(w_time[0], stage[1].astype(BF16))
    a_hid = a_hid + mm_nt(w_time[1], stage[2].astype(BF16))
    a_hid = a_hid + mm_nt(w_time[2], stage[3].astype(BF16))
    high = a_hid.astype(BF16).astype(F32)
    low = a_hid - high
    for u in range(PATCH):
        turn = (lambda m: m) if u == 0 else (lambda m: pltpu.roll(m, 3 * u, 1))
        wp[u, 0:C, 0:C] = turn(a_video).astype(BF16)
        wp[u, 0:C, C : 2 * C] = blank
        wp[u, C : 2 * C, 0:C] = turn(high).astype(BF16)
        wp[u, C : 2 * C, C : 2 * C] = turn(low).astype(BF16)
    for h in range(2):
        wpf[h] = w_patch[:, h * C : (h + 1) * C].astype(F32)
    for v in range(PATCH):
        taps = [wpf[h, pl.ds(v, 24, stride=PATCH), :] for h in range(2)]
        taps = jnp.concatenate(taps, axis=1)
        full = jnp.concatenate([taps, jnp.zeros((C - 24, 2 * C), F32)], axis=0)
        wv[v] = full.astype(BF16)

    acc[...] = jnp.zeros((12, C, C), F32)

    load_v.wait()
    load_g.wait()

    @pl.when(r > 0)
    def _():
        to_up.wait_send()
        to_down.wait_recv()

    @pl.when(r < nr - 1)
    def _():
        to_down.wait_send()
        to_up.wait_recv()

    col512 = lax.rem(lax.broadcasted_iota(jnp.int32, (512, 2 * C), 0), 128)
    col128 = lax.broadcasted_iota(jnp.int32, (128, C), 0)

    def conv(src, f, w, steps):
        lhs = jnp.concatenate(
            [
                jnp.concatenate([src[f, 2 * p + a] for p in range(4)], axis=0)
                for a in range(4)
            ],
            axis=1,
        )
        total = mm(lhs, w[1])
        total = total + shifted(mm(lhs, w[0]), col512, steps[0])
        return total + shifted(mm(lhs, w[2]), col512, steps[1])

    def edge_up(f):
        return remote(bpad.at[f, 1], bpad.at[f, rd + 1], bs.at[f, 0], br.at[f, 0], t, jnp.maximum(r - 1, 0))

    def edge_down(f):
        return remote(bpad.at[f, rd], bpad.at[f, 0], bs.at[f, 1], br.at[f, 1], t, jnp.minimum(r + 1, nr - 1))

    def pair(p, carry):
        f0 = 2 * p

        @pl.when(p == fd // 2 - 1)
        def _():
            @pl.when(t > 0)
            def _():
                to_prev.wait_send()

            @pl.when(t < nt - 1)
            def _():
                to_prev.wait_recv()

        lhs = jnp.concatenate([gpad[f0 + a].reshape(rd * width, C) for a in range(4)], axis=1)
        both = mm(lhs, wt[...])
        bh[0] = both[:, 0:C]
        bh[1] = both[:, C : 2 * C]
        for o in range(2):
            f = f0 + o
            pre = conv(vpad, f, wf, (-1, 1))
            for i in range(rd):
                x = pre[(i // 2) * 128 : (i // 2) * 128 + 128, (i % 2) * C : (i % 2) * C + C]
                s = 0.5 * jnp.tanh(0.5 * x) + 0.5
                h = x * s
                hid[f, i] = h.astype(BF16)
                b = bh[o, i * 128 : (i + 1) * 128, :] * (s + h * (1.0 - s))
                bb = b.astype(BF16)
                bpad[f, i + 1] = bb
                cells = slice(i * 128, (i + 1) * 128)
                bcat[o, cells, C : 2 * C] = bb
                bcat[o, cells, 0:C] = shifted(b, col128, 1).astype(BF16)
                bcat[o, cells, 2 * C : 3 * C] = shifted(b, col128, -1).astype(BF16)

            @pl.when(r > 0)
            def _():
                edge_up(f).start()

            @pl.when(r < nr - 1)
            def _():
                edge_down(f).start()

            for i in range(rd + 2):
                vtr[i * C : (i + 1) * C, :] = vpad[f, i].T
            lead = jnp.concatenate([gpad[f + k].reshape(rd * width, C) for k in range(3)], axis=1)
            turned = jnp.concatenate([hid[f, i].T for i in range(rd)], axis=1)
            tg = mm(turned, lead)
            for k in range(3):
                acc[9 + k] += tg[:, k * C : (k + 1) * C]
            rows_t = jnp.concatenate([vtr[i * C : (i + 3) * C, :] for i in range(rd)], axis=1)
            sg = mm(rows_t, bcat[o])
            for di in range(3):
                for dj in range(3):
                    acc[di * 3 + dj] += sg[di * C : (di + 1) * C, dj * C : (dj + 1) * C]
        return carry

    lax.fori_loop(0, fd // 2, pair, 0)

    def step1():
        return remote(
            acc.at[pl.ds(6 * (1 - core), 6)], buf1, s1s.at[0], s1r.at[0], t, partner
        )

    step1().start()

    y = None
    for u in range(PATCH):
        lhs = jnp.concatenate(
            [vpad[:, u + 1].reshape(fd * width, C), hid[:, u].reshape(fd * width, C)], axis=1
        )
        term = mm(lhs, wp[u])
        y = term if y is None else y + term
    yb[...] = (y[:, 0:C] + y[:, C : 2 * C]).reshape(fd, width, C)
    lane = lax.broadcasted_iota(jnp.int32, (width, C), 1)

    def group(m, g):
        return m if g == 0 else pltpu.roll(m, C - 24 * g, 1)

    first = group(yb[fd - 1], 2) + group(yb[fd - 2], 3)
    second = pltpu.roll(yb[fd - 1], 128 - 48, 1)
    hsend[...] = jnp.where(lane < 24, first, jnp.where(lane < 48, second, 0.0))
    halo = remote(hsend, hrecv, hs.at[0], hr.at[0], jnp.where(t < nt - 1, t + 1, t - 1), r)

    @pl.when(t < nt - 1)
    def _():
        halo.start()

    step1().wait()
    piece = 768 // nt
    half = acc[pl.ds(6 * core, 6)] + buf1[...]
    s1[...] = half.reshape(nt, piece, C)

    def step2(d):
        peer = lax.rem(t + d, nt)
        return remote(s1.at[peer], buf2.at[t], s2s.at[d], s2r.at[t], peer, r)

    def step2_in(d):
        peer = lax.rem(t + d, nt)
        return remote(s1.at[t], buf2.at[peer], s2s.at[d], s2r.at[peer], peer, r)

    for d in range(1, nt):
        step2(d).start()
    buf2[t] = s1[t]

    def finish_frame(f):
        @pl.when(r > 0)
        def _():
            edge_up(f).wait_send()
            edge_down(f).wait_recv()

        @pl.when(r < nr - 1)
        def _():
            edge_down(f).wait_send()
            edge_up(f).wait_recv()

        out = conv(bpad, f, wb, (1, -1))
        for i in range(rd):
            part = out[(i // 2) * 128 : (i // 2) * 128 + 128, (i % 2) * C : (i % 2) * C + C]
            og[f, i] = (gpad[f, i].astype(F32) + part).astype(BF16)
        pltpu.make_async_copy(og.at[f], out_ig.at[f], osem.at[f]).start()

    def frames(lo, hi):
        lax.fori_loop(lo, hi, lambda f, c: (finish_frame(f), c)[1], 0)

    frames(0, 3)

    @pl.when(t > 0)
    def _():
        halo.wait_recv()

    @pl.when(t < nt - 1)
    def _():
        halo.wait_send()

    lane8 = lax.broadcasted_iota(jnp.int32, (8, C), 1)
    sub8 = lax.broadcasted_iota(jnp.int32, (8, C), 0)
    count = 24.0 * width
    stats = jnp.zeros((8, C), F32)
    for f in range(fd):
        m = yb[f] + group(yb[f], 1)
        m = m + (group(yb[f - 1], 2) if f >= 1 else 0.0)
        m = m + (group(yb[f - 2], 3) if f >= 2 else 0.0)
        if f < 2:
            m = m + group(hrecv[...], f)
        m = jnp.where(lane < 24, m, 0.0).astype(BF16).astype(F32)
        pix[f * width : (f + 1) * width, :] = m
        mean = jnp.sum(m, keepdims=True) / count
        away = jnp.where(lane < 24, m - mean, 0.0)
        square = jnp.sum(away * away, keepdims=True)
        here = jnp.where(lane8 == 0, mean, jnp.where(lane8 == 1, square, 0.0))
        stats = stats + jnp.where(sub8 == f, here, 0.0)
    stat[r] = stats

    def stat_out(d):
        return remote(stat.at[r], stat.at[r], ss.at[d], sr.at[r], t, lax.rem(r + d, nr))

    def stat_in(d):
        peer = lax.rem(r + d, nr)
        return remote(stat.at[r], stat.at[peer], ss.at[d], sr.at[peer], t, peer)

    for d in range(1, nr):
        stat_out(d).start()

    frames(3, 5)

    for d in range(1, nt):
        step2(d).wait_send()
        step2_in(d).wait_recv()
    buf3[xpos] = jnp.sum(buf2[...], axis=0)

    def step3(d):
        return remote(
            buf3.at[xpos], buf3.at[xpos], s3s.at[d], s3r.at[xpos], t,
            2 * lax.rem(xpos + d, nx) + core,
        )

    def step3_in(d):
        peer = lax.rem(xpos + d, nx)
        return remote(
            buf3.at[xpos], buf3.at[peer], s3s.at[d], s3r.at[peer], t, 2 * peer + core
        )

    for d in range(1, nx):
        step3(d).start()

    for d in range(1, nr):
        stat_out(d).wait_send()
        stat_in(d).wait_recv()

    every = stat[...]
    means = jnp.sum(jnp.where(lane8 == 0, every, 0.0), axis=2, keepdims=True)
    squares = jnp.sum(jnp.where(lane8 == 1, every, 0.0), axis=2, keepdims=True)
    center = jnp.sum(means, axis=0, keepdims=True) / nr
    apart = means - center
    spread = jnp.sum(squares + count * apart * apart, axis=0, keepdims=True) / (count * nr)
    scale = lax.rsqrt(spread + 1e-05)
    for f in range(fd):
        m = pix[f * width : (f + 1) * width, :]
        m = (m - center[0, f : f + 1, :]) * scale[0, f : f + 1, :]
        pix[f * width : (f + 1) * width, :] = m
    inner = jnp.zeros((fd * width // PATCH, 2 * C), F32)
    for v in range(PATCH):
        taken = pix[pl.ds(v, fd * width // PATCH, stride=PATCH), :]
        inner = inner + mm(taken.astype(BF16), wv[v])
    inner = jnp.where(inner >= 0, inner, 0.2 * inner)
    in_high = inner.astype(BF16)
    in_low = (inner - in_high.astype(F32)).astype(BF16)
    wl = jnp.broadcast_to(w_logit[...], (8, 2 * C)).astype(BF16)
    lgs[r] = mm_nt(wl, in_high) + mm_nt(wl, in_low)

    def lg_out(d):
        return remote(lgs.at[r], lgs.at[r], ls.at[d], lr.at[r], t, lax.rem(r + d, nr))

    def lg_in(d):
        peer = lax.rem(r + d, nr)
        return remote(lgs.at[r], lgs.at[peer], ls.at[d], lr.at[peer], t, peer)

    for d in range(1, nr):
        lg_out(d).start()

    for d in range(1, nx):
        step3(d).wait_send()
        step3_in(d).wait_recv()
    ob[core, t] = jnp.sum(buf3[...], axis=0)

    def step4(d):
        return remote(ob.at[core, t], ob.at[core, t], s4s.at[d], s4r.at[t], lax.rem(t + d, nt), r)

    def step4_in(d):
        peer = lax.rem(t + d, nt)
        return remote(ob.at[core, t], ob.at[core, peer], s4s.at[d], s4r.at[peer], peer, r)

    for d in range(1, nt):
        step4(d).start()

    frames(5, 8)

    for d in range(1, nt):
        step4(d).wait_send()
        step4_in(d).wait_recv()
    step5 = remote(ob.at[core], ob.at[core], s5s.at[0], s5r.at[0], t, partner)
    step5_in = remote(ob.at[core], ob.at[1 - core], s5s.at[0], s5r.at[0], t, partner)
    step5.start()

    for d in range(1, nr):
        lg_out(d).wait_send()
        lg_in(d).wait_recv()
    table = jnp.concatenate([lgs[i, 0:1, :] for i in range(nr)], axis=0)
    out_lg[...] = pltpu.roll(table, lax.rem(C - 16 * r, C), 1)

    step5.wait_send()
    step5_in.wait_recv()
    out_ar[...] = ob[...]
    for f in range(fd):
        pltpu.make_async_copy(og.at[f], out_ig.at[f], osem.at[f]).wait()


def shards(video, w_space, w_time, w_pixel, w_patch, w_logit, grad_out):
    fd, rd, width, chans = video.shape
    nt = lax.axis_size("tm")
    nr = lax.axis_size("rows")
    hbm = pl.BlockSpec(memory_space=pl.ANY)
    vmem = pl.BlockSpec(memory_space=pltpu.VMEM)
    dma = pltpu.SemaphoreType.DMA
    piece = 768 // nt
    scratch = [
        pltpu.VMEM((fd, rd + 2, width, chans), BF16),
        pltpu.VMEM((fd + 2, rd, width, chans), BF16),
        pltpu.VMEM((fd, rd, width, chans), BF16),
        pltpu.VMEM((fd, rd + 2, width, chans), BF16),
        pltpu.VMEM((2, rd * width, 3 * chans), BF16),
        pltpu.VMEM(((rd + 2) * chans, width), BF16),
        pltpu.VMEM((2, rd * width, chans), F32),
        pltpu.VMEM((fd, rd, width, chans), BF16),
        pltpu.VMEM((3, 4 * chans, 2 * chans), BF16),
        pltpu.VMEM((3, 4 * chans, 2 * chans), BF16),
        pltpu.VMEM((4 * chans, 2 * chans), BF16),
        pltpu.VMEM((PATCH, 2 * chans, 2 * chans), BF16),
        pltpu.VMEM((2, 192, chans), F32),
        pltpu.VMEM((PATCH, chans, 2 * chans), BF16),
        pltpu.VMEM((4, chans, chans), F32),
        pltpu.VMEM((fd, width, chans), F32),
        pltpu.VMEM((width, chans), F32),
        pltpu.VMEM((width, chans), F32),
        pltpu.VMEM((nr, 8, chans), F32),
        pltpu.VMEM((nr, 8, chans), F32),
        pltpu.VMEM((fd * width, chans), F32),
        pltpu.VMEM((12, chans, chans), F32),
        pltpu.VMEM((6, chans, chans), F32),
        pltpu.VMEM((nt, piece, chans), F32),
        pltpu.VMEM((nt, piece, chans), F32),
        pltpu.VMEM((nr // 2, piece, chans), F32),
        pltpu.VMEM((2, nt, piece, chans), F32),
        dma((2,)), dma((fd,)),
        dma((2,)), dma((2,)), dma((1,)), dma((1,)), dma((fd, 2)), dma((fd, 2)),
        dma((1,)), dma((1,)), dma((nr,)), dma((nr,)), dma((nr,)), dma((nr,)),
        dma((1,)), dma((1,)), dma((nt,)), dma((nt,)), dma((nr // 2,)), dma((nr // 2,)),
        dma((nt,)), dma((nt,)), dma((1,)), dma((1,)),
    ]
    ig, ar, lg = pl.pallas_call(
        functools.partial(kernel, nt, nr),
        out_shape=(
            jax.ShapeDtypeStruct(video.shape, BF16),
            jax.ShapeDtypeStruct((2, nt, piece, chans), F32),
            jax.ShapeDtypeStruct((nr, chans), F32),
        ),
        in_specs=[hbm, vmem, vmem, vmem, vmem, vmem, hbm],
        out_specs=(hbm, vmem, vmem),
        scratch_shapes=scratch,
        compiler_params=pltpu.CompilerParams(
            collective_id=0, has_side_effects=True, vmem_limit_bytes=56 * 1024 * 1024
        ),
        cost_estimate=pl.CostEstimate(
            flops=2 * fd * rd * width * chans * chans * 36,
            bytes_accessed=3 * fd * rd * width * chans * 2,
            transcendentals=fd * rd * width * chans,
        ),
        name="block_step",
    )(video, w_space, w_time, w_pixel, w_patch, w_logit.reshape(1, 2 * chans), grad_out)
    sums = ar.reshape(12, chans, chans) * (1.0 / math.sqrt(fd * rd * width * nt * nr))
    logits = lg[:, 0:16].reshape(1, nr, 16)
    return (ig, sums[0:9].reshape(3, 3, chans, chans), sums[9:12], logits)


def solution(mesh):
    in_specs = (P("tm", "rows", None, None), P(), P(), P(), P(), P(), P("tm", "rows", None, None))
    out_specs = (P("tm", "rows", None, None), P(), P(), P(("tm", "rows"), None, None))
    return jax.shard_map(shards, mesh=mesh, in_specs=in_specs, out_specs=out_specs, check_vma=False)
```

```python
import functools
import math

import jax
import jax.numpy as jnp
from jax import lax
from jax.experimental import pallas as pl
from jax.experimental.pallas import tpu as pltpu
from jax.sharding import PartitionSpec as P

PATCH = 8
C = 128
LINE = C + 16
MESH = pl.DeviceIdType.MESH
F32 = jnp.float32
BF16 = jnp.bfloat16


def mm(a, b):
    return jnp.dot(a, b, preferred_element_type=F32)


def mm_nt(a, b):
    return lax.dot_general(a, b, (((1,), (1,)), ((), ())), preferred_element_type=F32)


def kernel(
    nt, nr, factor,
    video, w_space_in, w_time_in, w_pixel_in, w_patch_in, w_logit_in, grad,
    out_ig, out_sg, out_tg, out_lg,
    vpad, gpad, hid, bpad, bleft, bright, vtr, htr, bh, og,
    za, zb, line_a, line_b, ya, yb2,
    wf, wb, wt, wp, wpf, wv, stage,
    w_space, w_time, w_pixel, w_patch, w_logit,
    yb, hsend, hrecv, stat, lgs, pix,
    acc, pair, s1, s2, s3, ob,
    lsem, osem, wsem,
    vs, vr, gs, gr, bs, br, hs, hr, ss, sr, ls, lr,
    s1s, s1r, s2s, s2r, s3s, s3r, s4s, s4r, s5s, s5r,
):
    t = lax.axis_index("tm")
    r = lax.axis_index("rows")
    core = lax.rem(r, 2)
    xpos = r // 2
    nx = nr // 2
    partner = r + 1 - 2 * core
    fd, rd, width, _ = video.shape
    above = jnp.maximum(r - 1, 0)
    below = jnp.minimum(r + 1, nr - 1)

    def remote(src, dst, ssem, rsem, tt, rr):
        return pltpu.make_async_remote_copy(
            src_ref=src, dst_ref=dst, send_sem=ssem, recv_sem=rsem,
            device_id=(tt, rr), device_id_type=MESH,
        )

    barrier = pltpu.get_barrier_semaphore()
    for d in range(1, nr):
        pl.semaphore_signal(barrier, inc=1, device_id=(t, lax.rem(r + d, nr)), device_id_type=MESH)
    for d in range(1, nt):
        pl.semaphore_signal(barrier, inc=1, device_id=(lax.rem(t + d, nt), r), device_id_type=MESH)

    weights = ((w_space_in, w_space), (w_time_in, w_time), (w_pixel_in, w_pixel),
               (w_patch_in, w_patch), (w_logit_in, w_logit))
    loads = [pltpu.make_async_copy(a, b, wsem.at[i]) for i, (a, b) in enumerate(weights)]
    for load in loads:
        load.start()
    load_g = pltpu.make_async_copy(grad, gpad.at[0:fd], lsem.at[1])
    load_v = pltpu.make_async_copy(video, vpad.at[:, 1 : rd + 1], lsem.at[0])
    load_g.start()
    load_v.start()

    edge = jnp.zeros((8, C), F32)
    for z in (za, zb, ya, yb2):
        for dj in range(3):
            for q in range(z.shape[1]):
                z[dj, q, 0:8] = edge
                z[dj, q, C + 8 : LINE] = edge
    for z in (line_a, line_b):
        for q in range(4):
            z[q, 0:8] = edge
            z[q, C + 8 : LINE] = edge

    for load in loads:
        load.wait()

    blank = jnp.zeros((C, C), BF16)
    for a in range(4):
        for o in range(2):
            at = (slice(a * C, (a + 1) * C), slice(o * C, (o + 1) * C))
            lag = a - o
            wt[at] = w_time[lag].T * 0.5 if 0 <= lag <= 2 else blank
            for dj in range(3):
                wf[(dj,) + at] = w_space[lag, dj] * 0.5 if 0 <= lag <= 2 else blank

    pl.semaphore_wait(barrier, nr - 1 + nt - 1)

    parts = (pl.ds(0, 3), pl.ds(3, fd - 3))
    to_up = [
        remote(video.at[at, 0], vpad.at[at, rd + 1], vs.at[0, e], vr.at[0, e], t, above)
        for e, at in enumerate(parts)
    ]
    to_down = [
        remote(video.at[at, rd - 1], vpad.at[at, 0], vs.at[1, e], vr.at[1, e], t, below)
        for e, at in enumerate(parts)
    ]
    to_prev = remote(grad.at[0:2], gpad.at[fd : fd + 2], gs.at[0], gr.at[0], jnp.maximum(t - 1, 0), r)

    for e in range(2):
        @pl.when(r > 0)
        def _():
            to_up[e].start()

        @pl.when(r < nr - 1)
        def _():
            to_down[e].start()

    @pl.when(t > 0)
    def _():
        to_prev.start()

    @pl.when(r == 0)
    def _():
        vpad[:, 0] = jnp.zeros((fd, width, C), BF16)
        bpad[:, 0] = jnp.zeros((fd, width, C), BF16)

    @pl.when(r == nr - 1)
    def _():
        vpad[:, rd + 1] = jnp.zeros((fd, width, C), BF16)
        bpad[:, rd + 1] = jnp.zeros((fd, width, C), BF16)

    @pl.when(t == nt - 1)
    def _():
        gpad[fd : fd + 2] = jnp.zeros((2, rd, width, C), BF16)

    @pl.when(t == 0)
    def _():
        hrecv[...] = jnp.zeros((width, C), F32)

    def back_hidden(f0):
        lhs = jnp.concatenate([gpad[f0 + a].reshape(rd * width, C) for a in range(4)], axis=1)
        both = mm(lhs, wt[...])
        bh[f0] = both[:, 0:C]
        bh[f0 + 1] = both[:, C : 2 * C]

    load_g.wait()
    for f0 in range(0, fd - 2, 2):
        back_hidden(f0)

    load_v.wait()

    def taps(src, f, starts, w, z):
        lhs = jnp.concatenate(
            [jnp.concatenate([src[f, 2 * p + a] for p in starts], axis=0) for a in range(4)], axis=1
        )
        for dj in range(3):
            part = mm(lhs, w[dj])
            for k in range(len(starts)):
                for o in range(2):
                    z[dj, 2 * k + o, 8 : C + 8] = part[k * C : (k + 1) * C, o * C : (o + 1) * C]

    def joined(z, q, steps):
        mid = z[1, q, 8 : C + 8]
        return mid + z[0, q, 8 + steps[0] : C + 8 + steps[0]] + z[2, q, 8 + steps[1] : C + 8 + steps[1]]

    groups = ((0, fd - 2), (fd - 2, 2))

    def edge_up(g):
        at = pl.ds(*groups[g])
        return remote(bpad.at[at, 1], bpad.at[at, rd + 1], bs.at[g, 0], br.at[g, 0], t, above)

    def edge_down(g):
        at = pl.ds(*groups[g])
        return remote(bpad.at[at, rd], bpad.at[at, 0], bs.at[g, 1], br.at[g, 1], t, below)

    def send_edges(g):
        @pl.when(r > 0)
        def _():
            edge_up(g).start()

        @pl.when(r < nr - 1)
        def _():
            edge_down(g).start()

    late = fd - 2
    units = 2 * fd

    def place(u):
        last = u // (2 * late)
        f = (1 - last) * lax.rem(u, late) + last * (late + lax.rem(u, 2))
        outer = (1 - last) * (u // late) + last * lax.rem(u // 2, 2)
        return f, outer, (1 - outer, 2 + outer)

    def forward(u, z):
        f, _, starts = place(u)
        taps(vpad, f, starts, wf, z)

    def activate(u, z, line):
        f, outer, starts = place(u)
        for k in range(2):
            for o in range(2):
                q = 2 * k + o
                i = 2 * starts[k] + o
                x = joined(z, q, (-1, 1))
                th = jnp.tanh(x)
                up = 1.0 + th
                h = x * up
                hb = h.astype(BF16)
                hid[f, i] = hb
                htr[f, i] = hb.T
                b = bh[f, pl.ds(i * C, C), :] * (up + h * (1.0 - th))
                line[q, 8 : C + 8] = b
                bpad[f, i + 1] = b.astype(BF16)
                bleft[f, i] = line[q, 9 : C + 9].astype(BF16)
                bright[f, i] = line[q, 7 : C + 7].astype(BF16)
                vtr[f, i + 1] = vpad[f, i + 1].T

        @pl.when(outer == 1)
        def _():
            vtr[f, 0] = vpad[f, 0].T
            vtr[f, rd + 1] = vpad[f, rd + 1].T

    def two_units(k, carry):
        forward(2 * k + 1, zb)
        activate(2 * k, za, line_a)

        for e in range(2):
            @pl.when(k == late // 2 - 1 + e)
            def _():
                @pl.when(r > 0)
                def _():
                    to_up[e].wait_send()
                    to_down[e].wait_recv()

                @pl.when(r < nr - 1)
                def _():
                    to_down[e].wait_send()
                    to_up[e].wait_recv()

        forward(jnp.minimum(2 * k + 2, units - 1), za)
        activate(2 * k + 1, zb, line_b)
        return carry

    mine = pl.ds(6 * core, 6)
    other = pl.ds(6 * (1 - core), 6)

    def sum1():
        return remote(acc.at[other], pair, s1s.at[0], s1r.at[0], t, partner)

    def sum2(d):
        peer = lax.rem(t + d, nt)
        return remote(s1.at[peer], s2.at[t], s2s.at[d], s2r.at[t], peer, r)

    def sum2_in(d):
        peer = lax.rem(t + d, nt)
        return remote(s1.at[t], s2.at[peer], s2s.at[d], s2r.at[peer], peer, r)

    def sum3(d):
        peer = lax.rem(xpos + d, nx)
        return remote(s3.at[xpos], s3.at[xpos], s3s.at[d], s3r.at[xpos], t, 2 * peer + core)

    def sum3_in(d):
        peer = lax.rem(xpos + d, nx)
        return remote(s3.at[xpos], s3.at[peer], s3s.at[d], s3r.at[peer], t, 2 * peer + core)

    def back4(d):
        return remote(
            ob.at[core, t], ob.at[core, t], s4s.at[d], s4r.at[t], lax.rem(t + d, nt), r
        )

    def back4_in(d):
        peer = lax.rem(t + d, nt)
        return remote(ob.at[core, t], ob.at[core, peer], s4s.at[d], s4r.at[peer], peer, r)

    back5 = remote(ob.at[core], ob.at[core], s5s.at[0], s5r.at[0], t, partner)
    back5_in = remote(ob.at[core], ob.at[1 - core], s5s.at[0], s5r.at[0], t, partner)

    def go2():
        sum1().wait()
        s1[...] = (acc[mine] + pair[...]).reshape(s1.shape).astype(s1.dtype)
        for d in range(1, nt):
            sum2(d).start()
        s2[t] = s1[t]

    def go3():
        for d in range(1, nt):
            sum2(d).wait_send()
            sum2_in(d).wait_recv()
        s3[xpos] = jnp.sum(s2[...].astype(F32), axis=0)
        for d in range(1, nx):
            sum3(d).start()

    def go4():
        for d in range(1, nx):
            sum3(d).wait_send()
            sum3_in(d).wait_recv()
        ob[core, t] = (jnp.sum(s3[...], axis=0) * factor).astype(BF16)
        for d in range(1, nt):
            back4(d).start()

    def go5():
        for d in range(1, nt):
            back4(d).wait_send()
            back4_in(d).wait_recv()
        back5.start()

    def finish_sums():
        back5.wait_send()
        back5_in.wait_recv()
        blocks = ob[...].reshape(12, C, C).astype(F32)
        for di in range(3):
            for dj in range(3):
                out_sg[di, dj] = blocks[3 * di + dj]
        for k in range(3):
            out_tg[k] = blocks[9 + k]

    acc[...] = jnp.zeros((12, C, C), F32)

    def cells(x, f):
        return jnp.concatenate([x[f], x[f + 1]], axis=0).reshape(2 * rd * width, C)

    def grads(h, carry):
        f = 2 * h
        lhs = jnp.concatenate(
            [vtr[f + e, i : i + 3].reshape(3 * C, width) for e in range(2) for i in range(rd)], axis=1
        )
        mid = jnp.concatenate([bpad[f + e, 1 : rd + 1] for e in range(2)], axis=0)
        rhs = jnp.concatenate(
            [cells(bleft, f), mid.reshape(2 * rd * width, C), cells(bright, f)], axis=1
        )
        sg = mm(lhs, rhs)
        for di in range(3):
            for dj in range(3):
                acc[3 * di + dj] += sg[di * C : (di + 1) * C, dj * C : (dj + 1) * C]
        lhs = jnp.concatenate([htr[f + e, i] for e in range(2) for i in range(rd)], axis=1)
        tg = mm(lhs, jnp.concatenate([cells(gpad, f + k) for k in range(3)], axis=1))
        for k in range(3):
            acc[9 + k] += tg[:, k * C : (k + 1) * C]
        return carry

    forward(0, za)
    lax.fori_loop(0, late, two_units, 0)
    send_edges(0)
    lax.fori_loop(0, late // 2, grads, 0)

    @pl.when(t > 0)
    def _():
        to_prev.wait_send()

    @pl.when(t < nt - 1)
    def _():
        to_prev.wait_recv()

    back_hidden(late)
    lax.fori_loop(late, units // 2, two_units, 0)
    send_edges(1)
    grads(late // 2, 0)
    sum1().start()

    stage[...] = jnp.zeros((4, C, C), F32)
    pixel_rows = w_pixel[...].astype(F32)
    for g in range(4):
        stage[g, 24 * g : 24 * g + 3, :] = pixel_rows
    eye = (
        lax.broadcasted_iota(jnp.int32, (C, C), 0) == lax.broadcasted_iota(jnp.int32, (C, C), 1)
    ).astype(BF16)
    a_video = mm_nt(eye, stage[0].astype(BF16))
    a_hid = mm_nt(w_time[0], stage[1].astype(BF16))
    a_hid = a_hid + mm_nt(w_time[1], stage[2].astype(BF16))
    a_hid = a_hid + mm_nt(w_time[2], stage[3].astype(BF16))
    high = a_hid.astype(BF16).astype(F32)
    low = a_hid - high
    for u in range(PATCH):
        turn = (lambda m: m) if u == 0 else (lambda m: pltpu.roll(m, 3 * u, 1))
        wp[u, 0:C, 0:C] = turn(a_video).astype(BF16)
        wp[u, 0:C, C : 2 * C] = blank
        wp[u, C : 2 * C, 0:C] = turn(high).astype(BF16)
        wp[u, C : 2 * C, C : 2 * C] = turn(low).astype(BF16)
    y = None
    for u in range(PATCH):
        lhs = jnp.concatenate(
            [vpad[:, u + 1].reshape(fd * width, C), hid[:, u].reshape(fd * width, C)], axis=1
        )
        term = mm(lhs, wp[u])
        y = term if y is None else y + term
    yb[...] = (y[:, 0:C] + y[:, C : 2 * C]).reshape(fd, width, C)
    lane = lax.broadcasted_iota(jnp.int32, (width, C), 1)

    def group(m, g):
        return m if g == 0 else pltpu.roll(m, C - 24 * g, 1)

    first = group(yb[fd - 1], 2) + group(yb[fd - 2], 3)
    second = pltpu.roll(yb[fd - 1], 128 - 48, 1)
    hsend[...] = jnp.where(lane < 24, first, jnp.where(lane < 48, second, 0.0))
    halo = remote(hsend, hrecv, hs.at[0], hr.at[0], jnp.where(t < nt - 1, t + 1, t - 1), r)

    @pl.when(t < nt - 1)
    def _():
        halo.start()

    for a in range(4):
        for o in range(2):
            at = (slice(a * C, (a + 1) * C), slice(o * C, (o + 1) * C))
            di = o + 2 - a
            for dj in range(3):
                wb[(dj,) + at] = w_space[di, dj].T if 0 <= di <= 2 else blank

    def arrived(g):
        @pl.when(r > 0)
        def _():
            edge_up(g).wait_send()
            edge_down(g).wait_recv()

        @pl.when(r < nr - 1)
        def _():
            edge_down(g).wait_send()
            edge_up(g).wait_recv()

    def frame_out(f):
        return pltpu.make_async_copy(og.at[f], out_ig.at[f], osem.at[f])

    def backward(f, z):
        taps(bpad, f, range(rd // 2), wb, z)

    def settle(f, z):
        for i in range(rd):
            og[f, i] = (gpad[f, i].astype(F32) + joined(z, i, (1, -1))).astype(BF16)

    def frame(f):
        if f == fd - 3:
            arrived(1)
        if f < fd - 1:
            backward(f + 1, (ya, yb2)[(f + 1) % 2])
        settle(f, (ya, yb2)[f % 2])
        frame_out(f).start()

    arrived(0)
    backward(0, ya)
    go2()
    frame(0)
    frame(1)

    @pl.when(t > 0)
    def _():
        halo.wait_recv()

    @pl.when(t < nt - 1)
    def _():
        halo.wait_send()

    lane8 = lax.broadcasted_iota(jnp.int32, (8, C), 1)
    sub8 = lax.broadcasted_iota(jnp.int32, (8, C), 0)
    count = 24.0 * width
    stats = jnp.zeros((8, C), F32)
    for f in range(fd):
        m = yb[f] + group(yb[f], 1)
        m = m + (group(yb[f - 1], 2) if f >= 1 else 0.0)
        m = m + (group(yb[f - 2], 3) if f >= 2 else 0.0)
        if f < 2:
            m = m + group(hrecv[...], f)
        m = jnp.where(lane < 24, m, 0.0).astype(BF16).astype(F32)
        pix[f * width : (f + 1) * width, :] = m
        mean = jnp.sum(m, keepdims=True) / count
        away = jnp.where(lane < 24, m - mean, 0.0)
        square = jnp.sum(away * away, keepdims=True)
        here = jnp.where(lane8 == 0, mean, jnp.where(lane8 == 1, square, 0.0))
        stats = stats + jnp.where(sub8 == f, here, 0.0)
    stat[r] = stats

    def stat_out(d):
        return remote(stat.at[r], stat.at[r], ss.at[d], sr.at[r], t, lax.rem(r + d, nr))

    def stat_in(d):
        peer = lax.rem(r + d, nr)
        return remote(stat.at[r], stat.at[peer], ss.at[d], sr.at[peer], t, peer)

    for d in range(1, nr):
        stat_out(d).start()

    frame(2)
    go3()
    frame(3)
    frame(4)

    for d in range(1, nr):
        stat_out(d).wait_send()
        stat_in(d).wait_recv()

    for h in range(2):
        wpf[h] = w_patch[:, h * C : (h + 1) * C].astype(F32)
    for v in range(PATCH):
        tap = jnp.concatenate([wpf[h, pl.ds(v, 24, stride=PATCH), :] for h in range(2)], axis=1)
        wv[v] = jnp.concatenate([tap, jnp.zeros((C - 24, 2 * C), F32)], axis=0).astype(BF16)
    every = stat[...]
    means = jnp.sum(jnp.where(lane8 == 0, every, 0.0), axis=2, keepdims=True)
    squares = jnp.sum(jnp.where(lane8 == 1, every, 0.0), axis=2, keepdims=True)
    center = jnp.sum(means, axis=0, keepdims=True) / nr
    apart = means - center
    spread = jnp.sum(squares + count * apart * apart, axis=0, keepdims=True) / (count * nr)
    scale = lax.rsqrt(spread + 1e-05)
    for f in range(fd):
        m = pix[f * width : (f + 1) * width, :]
        m = (m - center[0, f : f + 1, :]) * scale[0, f : f + 1, :]
        pix[f * width : (f + 1) * width, :] = m
    inner = jnp.zeros((fd * width // PATCH, 2 * C), F32)
    for v in range(PATCH):
        taken = pix[pl.ds(v, fd * width // PATCH, stride=PATCH), :]
        inner = inner + mm(taken.astype(BF16), wv[v])
    inner = jnp.where(inner >= 0, inner, 0.2 * inner)
    in_high = inner.astype(BF16)
    in_low = (inner - in_high.astype(F32)).astype(BF16)
    wl = jnp.concatenate([w_logit[0:1], w_logit[1:2]], axis=1)
    wl = jnp.broadcast_to(wl, (8, 2 * C)).astype(BF16)
    lgs[r] = mm_nt(wl, in_high) + mm_nt(wl, in_low)

    def lg_out(d):
        return remote(lgs.at[r], lgs.at[r], ls.at[d], lr.at[r], t, lax.rem(r + d, nr))

    def lg_in(d):
        peer = lax.rem(r + d, nr)
        return remote(lgs.at[r], lgs.at[peer], ls.at[d], lr.at[peer], t, peer)

    for d in range(1, nr):
        lg_out(d).start()

    go4()
    frame(5)
    frame(6)
    frame(7)
    go5()

    for d in range(1, nr):
        lg_out(d).wait_send()
        lg_in(d).wait_recv()
    table = jnp.concatenate([lgs[i, 0:1, :] for i in range(nr)], axis=0)
    out_lg[0] = pltpu.roll(table, lax.rem(C - 16 * r, C), 1)[:, 0:16]

    finish_sums()
    for f in range(fd):
        frame_out(f).wait()


def hand_over(*refs):
    ins, outs, held, sem = refs[0:4], refs[4:8], refs[8:12], refs[12]
    fd = ins[0].shape[0]
    routes = [(ins[0].at[f], held[0].at[f], outs[0].at[f]) for f in range(fd)]
    routes += [(ins[i], held[i], outs[i]) for i in range(1, 4)]
    loads = [pltpu.make_async_copy(a, b, sem.at[0, i]) for i, (a, b, c) in enumerate(routes)]
    stores = [pltpu.make_async_copy(b, c, sem.at[1, i]) for i, (a, b, c) in enumerate(routes)]
    for load in loads:
        load.start()
    for load, store in zip(loads, stores):
        load.wait()
        store.start()
    for store in stores:
        store.wait()


def shards(video, w_space, w_time, w_pixel, w_patch, w_logit, grad_out):
    fd, rd, width, chans = video.shape
    nt = lax.axis_size("tm")
    nr = lax.axis_size("rows")
    hbm = pl.BlockSpec(memory_space=pltpu.HBM)
    vmem = pl.BlockSpec(memory_space=pltpu.VMEM)
    dma = pltpu.SemaphoreType.DMA
    piece = 6 * chans // nt
    scratch = [
        pltpu.VMEM((fd, rd + 2, width, chans), BF16),
        pltpu.VMEM((fd + 2, rd, width, chans), BF16),
        pltpu.VMEM((fd, rd, width, chans), BF16),
        pltpu.VMEM((fd, rd + 2, width, chans), BF16),
        pltpu.VMEM((fd, rd, width, chans), BF16),
        pltpu.VMEM((fd, rd, width, chans), BF16),
        pltpu.VMEM((fd, rd + 2, chans, width), BF16),
        pltpu.VMEM((fd, rd, chans, width), BF16),
        pltpu.VMEM((fd, rd * width, chans), F32),
        pltpu.VMEM((fd, rd, width, chans), BF16),
        pltpu.VMEM((3, 4, LINE, chans), F32),
        pltpu.VMEM((3, 4, LINE, chans), F32),
        pltpu.VMEM((4, LINE, chans), F32),
        pltpu.VMEM((4, LINE, chans), F32),
        pltpu.VMEM((3, rd, LINE, chans), F32),
        pltpu.VMEM((3, rd, LINE, chans), F32),
        pltpu.VMEM((3, 4 * chans, 2 * chans), BF16),
        pltpu.VMEM((3, 4 * chans, 2 * chans), BF16),
        pltpu.VMEM((4 * chans, 2 * chans), BF16),
        pltpu.VMEM((PATCH, 2 * chans, 2 * chans), BF16),
        pltpu.VMEM((2, 192, chans), F32),
        pltpu.VMEM((PATCH, chans, 2 * chans), BF16),
        pltpu.VMEM((4, chans, chans), F32),
        pltpu.VMEM((3, 3, chans, chans), BF16),
        pltpu.VMEM((3, chans, chans), BF16),
        pltpu.VMEM((3, chans), BF16),
        pltpu.VMEM((192, 2 * chans), BF16),
        pltpu.VMEM((2, chans), BF16),
        pltpu.VMEM((fd, width, chans), F32),
        pltpu.VMEM((width, chans), F32),
        pltpu.VMEM((width, chans), F32),
        pltpu.VMEM((nr, 8, chans), F32),
        pltpu.VMEM((nr, 8, chans), F32),
        pltpu.VMEM((fd * width, chans), F32),
        pltpu.VMEM((12, chans, chans), F32),
        pltpu.VMEM((6, chans, chans), F32),
        pltpu.VMEM((nt, piece, chans), BF16),
        pltpu.VMEM((nt, piece, chans), BF16),
        pltpu.VMEM((nr // 2, piece, chans), F32),
        pltpu.VMEM((2, nt, piece, chans), BF16),
        dma((2,)), dma((fd,)), dma((5,)),
        dma((2, 2)), dma((2, 2)), dma((1,)), dma((1,)), dma((2, 2)), dma((2, 2)),
        dma((1,)), dma((1,)), dma((nr,)), dma((nr,)), dma((nr,)), dma((nr,)),
        dma((1,)), dma((1,)), dma((nt,)), dma((nt,)), dma((nr // 2,)), dma((nr // 2,)),
        dma((nt,)), dma((nt,)), dma((1,)), dma((1,)),
    ]
    factor = 1.0 / math.sqrt(fd * rd * width * nt * nr)
    results = pl.pallas_call(
        functools.partial(kernel, nt, nr, factor),
        out_shape=(
            jax.ShapeDtypeStruct(video.shape, BF16),
            jax.ShapeDtypeStruct((3, 3, chans, chans), F32),
            jax.ShapeDtypeStruct((3, chans, chans), F32),
            jax.ShapeDtypeStruct((fd // nr, nr, width // PATCH), F32),
        ),
        in_specs=[hbm] * 7,
        out_specs=(pl.BlockSpec(memory_space=pl.ANY), vmem, vmem, vmem),
        scratch_shapes=scratch,
        compiler_params=pltpu.CompilerParams(
            collective_id=0, has_side_effects=True, vmem_limit_bytes=60 * 1024 * 1024
        ),
        cost_estimate=pl.CostEstimate(
            flops=2 * fd * rd * width * chans * chans * 36,
            bytes_accessed=3 * fd * rd * width * chans * 2,
            transcendentals=fd * rd * width * chans,
        ),
        name="block_step",
    )(video, w_space, w_time, w_pixel, w_patch, w_logit.reshape(2, chans), grad_out)
    anywhere = pl.BlockSpec(memory_space=pl.ANY)
    return pl.pallas_call(
        hand_over,
        out_shape=[jax.ShapeDtypeStruct(x.shape, x.dtype) for x in results],
        in_specs=[anywhere] * 4,
        out_specs=[anywhere] * 4,
        scratch_shapes=[pltpu.VMEM(x.shape, x.dtype) for x in results] + [dma((2, fd + 3))],
        name="hand_over",
    )(*results)


def solution(mesh):
    in_specs = (P("tm", "rows", None, None), P(), P(), P(), P(), P(), P("tm", "rows", None, None))
    out_specs = (P("tm", "rows", None, None), P(), P(), P(("tm", "rows"), None, None))
    return jax.shard_map(shards, mesh=mesh, in_specs=in_specs, out_specs=out_specs, check_vma=False)
```

```python
import functools
import math

import jax
import jax.numpy as jnp
from jax import lax
from jax.experimental import pallas as pl
from jax.experimental.pallas import tpu as pltpu
from jax.sharding import PartitionSpec as P

PATCH = 8
C = 128
LINE = C + 16
MESH = pl.DeviceIdType.MESH
F32 = jnp.float32
BF16 = jnp.bfloat16


def mm(a, b):
    return jnp.dot(a, b, preferred_element_type=F32)


def mm_nt(a, b):
    return lax.dot_general(a, b, (((1,), (1,)), ((), ())), preferred_element_type=F32)


def kernel(
    nt, nr, factor,
    video, w_space_in, w_time_in, w_pixel_in, w_patch_in, w_logit_in, grad,
    out_ig, out_sg, out_tg, out_lg,
    vpad, gpad, hid, bpad, bleft, bright, vtr, htr, bh, og,
    za, zb, line_a, line_b, ya, yb2,
    wf, wb, wt, wp, wpf, wv, stage,
    w_space, w_time, w_pixel, w_patch, w_logit,
    yb, hsend, hrecv, stat, lgs, pix,
    acc, pair, s1, s2, s3, ob,
    lsem, osem, wsem,
    vs, vr, gs, gr, bs, br, hs, hr, ss, sr, ls, lr,
    s1s, s1r, s2s, s2r, s3s, s3r, s4s, s4r, s5s, s5r,
):
    t = lax.axis_index("tm")
    r = lax.axis_index("rows")
    core = lax.rem(r, 2)
    xpos = r // 2
    nx = nr // 2
    partner = r + 1 - 2 * core
    fd, rd, width, _ = video.shape
    above = jnp.maximum(r - 1, 0)
    below = jnp.minimum(r + 1, nr - 1)

    def remote(src, dst, ssem, rsem, tt, rr):
        return pltpu.make_async_remote_copy(
            src_ref=src, dst_ref=dst, send_sem=ssem, recv_sem=rsem,
            device_id=(tt, rr), device_id_type=MESH,
        )

    barrier = pltpu.get_barrier_semaphore()
    for d in range(1, nr):
        pl.semaphore_signal(barrier, inc=1, device_id=(t, lax.rem(r + d, nr)), device_id_type=MESH)
    for d in range(1, nt):
        pl.semaphore_signal(barrier, inc=1, device_id=(lax.rem(t + d, nt), r), device_id_type=MESH)

    weights = ((w_space_in, w_space), (w_time_in, w_time), (w_pixel_in, w_pixel),
               (w_patch_in, w_patch), (w_logit_in, w_logit))
    loads = [pltpu.make_async_copy(a, b, wsem.at[i]) for i, (a, b) in enumerate(weights)]
    for load in loads:
        load.start()
    load_g = pltpu.make_async_copy(grad, gpad.at[0:fd], lsem.at[1])
    load_v = pltpu.make_async_copy(video, vpad.at[:, 1 : rd + 1], lsem.at[0])
    load_g.start()
    load_v.start()

    pl.semaphore_wait(barrier, nr - 1 + nt - 1)

    parts = (pl.ds(0, 3), pl.ds(3, fd - 3))
    to_up = [
        remote(video.at[at, 0], vpad.at[at, rd + 1], vs.at[0, e], vr.at[0, e], t, above)
        for e, at in enumerate(parts)
    ]
    to_down = [
        remote(video.at[at, rd - 1], vpad.at[at, 0], vs.at[1, e], vr.at[1, e], t, below)
        for e, at in enumerate(parts)
    ]
    to_prev = [
        remote(grad.at[e], gpad.at[fd + e], gs.at[e], gr.at[e], jnp.maximum(t - 1, 0), r)
        for e in range(2)
    ]

    for e in range(2):
        @pl.when(r > 0)
        def _():
            to_up[e].start()

        @pl.when(r < nr - 1)
        def _():
            to_down[e].start()

    @pl.when(t > 0)
    def _():
        to_prev[0].start()
        to_prev[1].start()


    edge = jnp.zeros((8, C), F32)
    for z in (za, zb, ya, yb2):
        for dj in range(3):
            for q in range(z.shape[1]):
                z[dj, q, 0:8] = edge
                z[dj, q, C + 8 : LINE] = edge
    for z in (line_a, line_b):
        for q in range(4):
            z[q, 0:8] = edge
            z[q, C + 8 : LINE] = edge

    for load in loads:
        load.wait()

    blank = jnp.zeros((C, C), BF16)
    for a in range(4):
        for o in range(2):
            at = (slice(a * C, (a + 1) * C), slice(o * C, (o + 1) * C))
            lag = a - o
            wt[at] = w_time[lag].T * 0.5 if 0 <= lag <= 2 else blank
            for dj in range(3):
                wf[(dj,) + at] = w_space[lag, dj] * 0.5 if 0 <= lag <= 2 else blank

    @pl.when(r == 0)
    def _():
        vpad[:, 0] = jnp.zeros((fd, width, C), BF16)
        bpad[:, 0] = jnp.zeros((fd, width, C), BF16)

    @pl.when(r == nr - 1)
    def _():
        vpad[:, rd + 1] = jnp.zeros((fd, width, C), BF16)
        bpad[:, rd + 1] = jnp.zeros((fd, width, C), BF16)

    @pl.when(t == nt - 1)
    def _():
        gpad[fd : fd + 2] = jnp.zeros((2, rd, width, C), BF16)

    @pl.when(t == 0)
    def _():
        hrecv[...] = jnp.zeros((width, C), F32)

    def back_hidden(f0):
        lhs = jnp.concatenate([gpad[f0 + a].reshape(rd * width, C) for a in range(4)], axis=1)
        both = mm(lhs, wt[...])
        bh[f0] = both[:, 0:C]
        bh[f0 + 1] = both[:, C : 2 * C]

    load_g.wait()
    for f0 in range(0, fd - 2, 2):
        back_hidden(f0)

    load_v.wait()

    def taps(src, f, starts, w, z):
        def tap(dj):
            lhs = jnp.concatenate(
                [jnp.concatenate([src[f, 2 * p + a] for p in starts], axis=0) for a in range(4)], axis=1
            )
            part = mm(lhs, w[dj])
            for k in range(len(starts)):
                for o in range(2):
                    z[dj, 2 * k + o, 8 : C + 8] = part[k * C : (k + 1) * C, o * C : (o + 1) * C]

        return [functools.partial(tap, dj) for dj in range(3)]

    def in_turns(first, second):
        count = len(first)
        for n, work in enumerate(first):
            work()
            for other in second[n * len(second) // count : (n + 1) * len(second) // count]:
                other()

    def joined(z, q, steps):
        mid = z[1, q, 8 : C + 8]
        return mid + z[0, q, 8 + steps[0] : C + 8 + steps[0]] + z[2, q, 8 + steps[1] : C + 8 + steps[1]]

    groups = ((0, fd - 2), (fd - 2, 2))

    def edge_up(g):
        at = pl.ds(*groups[g])
        return remote(bpad.at[at, 1], bpad.at[at, rd + 1], bs.at[g, 0], br.at[g, 0], t, above)

    def edge_down(g):
        at = pl.ds(*groups[g])
        return remote(bpad.at[at, rd], bpad.at[at, 0], bs.at[g, 1], br.at[g, 1], t, below)

    def send_edges(g):
        @pl.when(r > 0)
        def _():
            edge_up(g).start()

        @pl.when(r < nr - 1)
        def _():
            edge_down(g).start()

    late = fd - 2
    units = 2 * fd

    def place(u):
        last = u // (2 * late)
        f = (1 - last) * lax.rem(u, late) + last * (late + lax.rem(u // 2, 2))
        outer = (1 - last) * (u // late) + last * lax.rem(u, 2)
        return f, outer, (1 - outer, 2 + outer)

    def forward(u, z):
        f, _, starts = place(u)
        return taps(vpad, f, starts, wf, z)

    def activate(u, z, line):
        f, _, starts = place(u)

        def one(q):
            i = 2 * starts[q // 2] + q % 2
            x = joined(z, q, (-1, 1))
            th = jnp.tanh(x)
            up = 1.0 + th
            h = x * up
            hb = h.astype(BF16)
            hid[f, i] = hb
            htr[f, i] = hb.T
            b = bh[f, pl.ds(i * C, C), :] * (up + h * (1.0 - th))
            line[q, 8 : C + 8] = b
            bpad[f, i + 1] = b.astype(BF16)
            bleft[f, i] = line[q, 9 : C + 9].astype(BF16)
            bright[f, i] = line[q, 7 : C + 7].astype(BF16)
            vtr[f, i + 1] = vpad[f, i + 1].T

        return [functools.partial(one, q) for q in range(4)]

    def outer_rows(u):
        f, outer, _ = place(u)

        @pl.when(outer == 1)
        def _():
            vtr[f, 0] = vpad[f, 0].T
            vtr[f, rd + 1] = vpad[f, rd + 1].T

    def back_hidden_late(e):
        @pl.when(t > 0)
        def _():
            to_prev[e].wait_send()

        @pl.when(t < nt - 1)
        def _():
            to_prev[e].wait_recv()

        f = late + e
        lhs = jnp.concatenate([gpad[f + a].reshape(rd * width, C) for a in range(3)], axis=1)
        bh[f] = mm(lhs, wt[0 : 3 * C, 0:C])

    def two_units(k, carry):
        @pl.when(k == units // 2 - 1)
        def _():
            back_hidden_late(1)

        in_turns(forward(2 * k + 1, zb), activate(2 * k, za, line_a))
        outer_rows(2 * k)

        for e in range(2):
            @pl.when(k == late // 2 - 1 + e)
            def _():
                @pl.when(r > 0)
                def _():
                    to_up[e].wait_send()
                    to_down[e].wait_recv()

                @pl.when(r < nr - 1)
                def _():
                    to_down[e].wait_send()
                    to_up[e].wait_recv()

        in_turns(
            forward(jnp.minimum(2 * k + 2, units - 1), za), activate(2 * k + 1, zb, line_b)
        )
        outer_rows(2 * k + 1)
        return carry

    mine = pl.ds(6 * core, 6)
    other = pl.ds(6 * (1 - core), 6)

    def sum1():
        return remote(acc.at[other], pair, s1s.at[0], s1r.at[0], t, partner)

    def sum2(d):
        peer = lax.rem(t + d, nt)
        return remote(s1.at[peer], s2.at[t], s2s.at[0], s2r.at[0], peer, r)

    all2 = remote(s1.at[0 : nt - 1], s2.at[0 : nt - 1], s2s.at[0], s2r.at[0], t, partner)

    def sum3(d):
        peer = lax.rem(xpos + d, nx)
        return remote(s3.at[xpos], s3.at[xpos], s3s.at[0], s3r.at[0], t, 2 * peer + core)

    all3 = remote(s3.at[0 : nx - 1], s3.at[0 : nx - 1], s3s.at[0], s3r.at[0], t, partner)

    def back4(d):
        return remote(
            ob.at[core, t], ob.at[core, t], s4s.at[0], s4r.at[0], lax.rem(t + d, nt), r
        )

    all4 = remote(ob.at[core, 0 : nt - 1], ob.at[core, 0 : nt - 1], s4s.at[0], s4r.at[0], t, partner)

    back5 = remote(ob.at[core], ob.at[core], s5s.at[0], s5r.at[0], t, partner)
    back5_in = remote(ob.at[core], ob.at[1 - core], s5s.at[0], s5r.at[0], t, partner)

    def go2():
        sum1().wait()
        s1[...] = (acc[mine] + pair[...]).reshape(s1.shape).astype(s1.dtype)
        for d in range(1, nt):
            sum2(d).start()
        s2[t] = s1[t]

    def go3():
        all2.wait_recv()
        s3[xpos] = jnp.sum(s2[...].astype(F32), axis=0)
        for d in range(1, nx):
            sum3(d).start()

    def go4():
        all3.wait_recv()
        ob[core, t] = (jnp.sum(s3[...], axis=0) * factor).astype(BF16)
        for d in range(1, nt):
            back4(d).start()

    def go5():
        all4.wait_recv()
        back5.start()

    def finish_sums():
        back5.wait_send()
        back5_in.wait_recv()
        blocks = ob[...].reshape(12, C, C).astype(F32)
        for di in range(3):
            for dj in range(3):
                out_sg[di, dj] = blocks[3 * di + dj]
        for k in range(3):
            out_tg[k] = blocks[9 + k]

    acc[...] = jnp.zeros((12, C, C), F32)

    def cells(x, f):
        return jnp.concatenate([x[f], x[f + 1]], axis=0).reshape(2 * rd * width, C)

    def grads(h, carry):
        f = 2 * h
        lhs = jnp.concatenate(
            [vtr[f + e, i : i + 3].reshape(3 * C, width) for e in range(2) for i in range(rd)], axis=1
        )
        mid = jnp.concatenate([bpad[f + e, 1 : rd + 1] for e in range(2)], axis=0)
        rhs = jnp.concatenate(
            [cells(bleft, f), mid.reshape(2 * rd * width, C), cells(bright, f)], axis=1
        )
        sg = mm(lhs, rhs)
        for di in range(3):
            for dj in range(3):
                acc[3 * di + dj] += sg[di * C : (di + 1) * C, dj * C : (dj + 1) * C]
        lhs = jnp.concatenate([htr[f + e, i] for e in range(2) for i in range(rd)], axis=1)
        tg = mm(lhs, jnp.concatenate([cells(gpad, f + k) for k in range(3)], axis=1))
        for k in range(3):
            acc[9 + k] += tg[:, k * C : (k + 1) * C]
        return carry

    in_turns(forward(0, za), [])
    lax.fori_loop(0, late, two_units, 0)
    send_edges(0)
    lax.fori_loop(0, late // 2, grads, 0)

    back_hidden_late(0)
    lax.fori_loop(late, units // 2, two_units, 0)
    send_edges(1)
    grads(late // 2, 0)
    sum1().start()

    stage[...] = jnp.zeros((4, C, C), F32)
    pixel_rows = w_pixel[...].astype(F32)
    for g in range(4):
        stage[g, 24 * g : 24 * g + 3, :] = pixel_rows
    eye = (
        lax.broadcasted_iota(jnp.int32, (C, C), 0) == lax.broadcasted_iota(jnp.int32, (C, C), 1)
    ).astype(BF16)
    a_video = mm_nt(eye, stage[0].astype(BF16))
    a_hid = mm_nt(w_time[0], stage[1].astype(BF16))
    a_hid = a_hid + mm_nt(w_time[1], stage[2].astype(BF16))
    a_hid = a_hid + mm_nt(w_time[2], stage[3].astype(BF16))
    high = a_hid.astype(BF16).astype(F32)
    low = a_hid - high
    for u in range(PATCH):
        turn = (lambda m: m) if u == 0 else (lambda m: pltpu.roll(m, 3 * u, 1))
        wp[u, 0:C, 0:C] = turn(a_video).astype(BF16)
        wp[u, 0:C, C : 2 * C] = blank
        wp[u, C : 2 * C, 0:C] = turn(high).astype(BF16)
        wp[u, C : 2 * C, C : 2 * C] = turn(low).astype(BF16)
    y = None
    for u in range(PATCH):
        lhs = jnp.concatenate(
            [vpad[:, u + 1].reshape(fd * width, C), hid[:, u].reshape(fd * width, C)], axis=1
        )
        term = mm(lhs, wp[u])
        y = term if y is None else y + term
    yb[...] = (y[:, 0:C] + y[:, C : 2 * C]).reshape(fd, width, C)
    lane = lax.broadcasted_iota(jnp.int32, (width, C), 1)

    def group(m, g):
        return m if g == 0 else pltpu.roll(m, C - 24 * g, 1)

    first = group(yb[fd - 1], 2) + group(yb[fd - 2], 3)
    second = pltpu.roll(yb[fd - 1], 128 - 48, 1)
    hsend[...] = jnp.where(lane < 24, first, jnp.where(lane < 48, second, 0.0))
    halo = remote(hsend, hrecv, hs.at[0], hr.at[0], jnp.where(t < nt - 1, t + 1, t - 1), r)

    @pl.when(t < nt - 1)
    def _():
        halo.start()

    for a in range(4):
        for o in range(2):
            at = (slice(a * C, (a + 1) * C), slice(o * C, (o + 1) * C))
            di = o + 2 - a
            for dj in range(3):
                wb[(dj,) + at] = w_space[di, dj].T if 0 <= di <= 2 else blank

    def arrived(g):
        @pl.when(r > 0)
        def _():
            edge_up(g).wait_send()
            edge_down(g).wait_recv()

        @pl.when(r < nr - 1)
        def _():
            edge_down(g).wait_send()
            edge_up(g).wait_recv()

    def frame_out(f):
        return pltpu.make_async_copy(og.at[f], out_ig.at[f], osem.at[f])

    def backward(f, z):
        return taps(bpad, f, range(rd // 2), wb, z)

    def settle(f, z):
        def one(i):
            og[f, i] = (gpad[f, i].astype(F32) + joined(z, i, (1, -1))).astype(BF16)

        return [functools.partial(one, i) for i in range(rd)]

    def frame(f):
        if f == fd - 3:
            arrived(1)
        lines = settle(f, (ya, yb2)[f % 2])
        if f < fd - 1:
            in_turns(backward(f + 1, (ya, yb2)[(f + 1) % 2]), lines)
        else:
            for line in lines:
                line()
        frame_out(f).start()

    arrived(0)
    in_turns(backward(0, ya), [])
    go2()
    frame(0)
    frame(1)

    @pl.when(t > 0)
    def _():
        halo.wait_recv()

    @pl.when(t < nt - 1)
    def _():
        halo.wait_send()

    lane8 = lax.broadcasted_iota(jnp.int32, (8, C), 1)
    sub8 = lax.broadcasted_iota(jnp.int32, (8, C), 0)
    count = 24.0 * width
    stats = jnp.zeros((8, C), F32)
    for f in range(fd):
        m = yb[f] + group(yb[f], 1)
        m = m + (group(yb[f - 1], 2) if f >= 1 else 0.0)
        m = m + (group(yb[f - 2], 3) if f >= 2 else 0.0)
        if f < 2:
            m = m + group(hrecv[...], f)
        m = jnp.where(lane < 24, m, 0.0).astype(BF16).astype(F32)
        pix[f * width : (f + 1) * width, :] = m
        mean = jnp.sum(m, keepdims=True) / count
        away = jnp.where(lane < 24, m - mean, 0.0)
        square = jnp.sum(away * away, keepdims=True)
        here = jnp.where(lane8 == 0, mean, jnp.where(lane8 == 1, square, 0.0))
        stats = stats + jnp.where(sub8 == f, here, 0.0)
    stat[r] = stats

    def stat_out(d):
        return remote(stat.at[r], stat.at[r], ss.at[0], sr.at[0], t, lax.rem(r + d, nr))

    all_stat = remote(stat.at[0 : nr - 1], stat.at[0 : nr - 1], ss.at[0], sr.at[0], t, partner)

    for d in range(1, nr):
        stat_out(d).start()

    frame(2)
    go3()
    frame(3)
    frame(4)

    all_stat.wait_recv()

    for h in range(2):
        wpf[h] = w_patch[:, h * C : (h + 1) * C].astype(F32)
    for v in range(PATCH):
        tap = jnp.concatenate([wpf[h, pl.ds(v, 24, stride=PATCH), :] for h in range(2)], axis=1)
        wv[v] = jnp.concatenate([tap, jnp.zeros((C - 24, 2 * C), F32)], axis=0).astype(BF16)
    every = stat[...]
    means = jnp.sum(jnp.where(lane8 == 0, every, 0.0), axis=2, keepdims=True)
    squares = jnp.sum(jnp.where(lane8 == 1, every, 0.0), axis=2, keepdims=True)
    center = jnp.sum(means, axis=0, keepdims=True) / nr
    apart = means - center
    spread = jnp.sum(squares + count * apart * apart, axis=0, keepdims=True) / (count * nr)
    scale = lax.rsqrt(spread + 1e-05)
    for f in range(fd):
        m = pix[f * width : (f + 1) * width, :]
        m = (m - center[0, f : f + 1, :]) * scale[0, f : f + 1, :]
        pix[f * width : (f + 1) * width, :] = m
    inner = jnp.zeros((fd * width // PATCH, 2 * C), F32)
    for v in range(PATCH):
        taken = pix[pl.ds(v, fd * width // PATCH, stride=PATCH), :]
        inner = inner + mm(taken.astype(BF16), wv[v])
    inner = jnp.where(inner >= 0, inner, 0.2 * inner)
    in_high = inner.astype(BF16)
    in_low = (inner - in_high.astype(F32)).astype(BF16)
    wl = jnp.concatenate([w_logit[0:1], w_logit[1:2]], axis=1)
    wl = jnp.broadcast_to(wl, (8, 2 * C)).astype(BF16)
    lgs[r] = mm_nt(wl, in_high) + mm_nt(wl, in_low)

    def lg_out(d):
        return remote(lgs.at[r], lgs.at[r], ls.at[0], lr.at[0], t, lax.rem(r + d, nr))

    all_lg = remote(lgs.at[0 : nr - 1], lgs.at[0 : nr - 1], ls.at[0], lr.at[0], t, partner)

    for d in range(1, nr):
        lg_out(d).start()

    go4()
    frame(5)
    frame(6)
    frame(7)
    go5()

    all_lg.wait_recv()
    table = jnp.concatenate([lgs[i, 0:1, :] for i in range(nr)], axis=0)
    out_lg[0] = pltpu.roll(table, lax.rem(C - 16 * r, C), 1)[:, 0:16]

    finish_sums()
    for step in (all2, all3, all4, all_stat, all_lg):
        step.wait_send()
    for f in range(fd):
        frame_out(f).wait()


def hand_over(*refs):
    ins, outs, held, sem = refs[0:4], refs[4:8], refs[8:12], refs[12]
    fd = ins[0].shape[0]
    routes = [(ins[0].at[f], held[0].at[f], outs[0].at[f]) for f in range(fd)]
    routes += [(ins[i], held[i], outs[i]) for i in range(1, 4)]
    loads = [pltpu.make_async_copy(a, b, sem.at[0, i]) for i, (a, b, c) in enumerate(routes)]
    stores = [pltpu.make_async_copy(b, c, sem.at[1, i]) for i, (a, b, c) in enumerate(routes)]
    for load in loads:
        load.start()
    for load, store in zip(loads, stores):
        load.wait()
        store.start()
    for store in stores:
        store.wait()


def shards(video, w_space, w_time, w_pixel, w_patch, w_logit, grad_out):
    fd, rd, width, chans = video.shape
    nt = lax.axis_size("tm")
    nr = lax.axis_size("rows")
    hbm = pl.BlockSpec(memory_space=pltpu.HBM)
    vmem = pl.BlockSpec(memory_space=pltpu.VMEM)
    dma = pltpu.SemaphoreType.DMA
    piece = 6 * chans // nt
    scratch = [
        pltpu.VMEM((fd, rd + 2, width, chans), BF16),
        pltpu.VMEM((fd + 2, rd, width, chans), BF16),
        pltpu.VMEM((fd, rd, width, chans), BF16),
        pltpu.VMEM((fd, rd + 2, width, chans), BF16),
        pltpu.VMEM((fd, rd, width, chans), BF16),
        pltpu.VMEM((fd, rd, width, chans), BF16),
        pltpu.VMEM((fd, rd + 2, chans, width), BF16),
        pltpu.VMEM((fd, rd, chans, width), BF16),
        pltpu.VMEM((fd, rd * width, chans), F32),
        pltpu.VMEM((fd, rd, width, chans), BF16),
        pltpu.VMEM((3, 4, LINE, chans), F32),
        pltpu.VMEM((3, 4, LINE, chans), F32),
        pltpu.VMEM((4, LINE, chans), F32),
        pltpu.VMEM((4, LINE, chans), F32),
        pltpu.VMEM((3, rd, LINE, chans), F32),
        pltpu.VMEM((3, rd, LINE, chans), F32),
        pltpu.VMEM((3, 4 * chans, 2 * chans), BF16),
        pltpu.VMEM((3, 4 * chans, 2 * chans), BF16),
        pltpu.VMEM((4 * chans, 2 * chans), BF16),
        pltpu.VMEM((PATCH, 2 * chans, 2 * chans), BF16),
        pltpu.VMEM((2, 192, chans), F32),
        pltpu.VMEM((PATCH, chans, 2 * chans), BF16),
        pltpu.VMEM((4, chans, chans), F32),
        pltpu.VMEM((3, 3, chans, chans), BF16),
        pltpu.VMEM((3, chans, chans), BF16),
        pltpu.VMEM((3, chans), BF16),
        pltpu.VMEM((192, 2 * chans), BF16),
        pltpu.VMEM((2, chans), BF16),
        pltpu.VMEM((fd, width, chans), F32),
        pltpu.VMEM((width, chans), F32),
        pltpu.VMEM((width, chans), F32),
        pltpu.VMEM((nr, 8, chans), F32),
        pltpu.VMEM((nr, 8, chans), F32),
        pltpu.VMEM((fd * width, chans), F32),
        pltpu.VMEM((12, chans, chans), F32),
        pltpu.VMEM((6, chans, chans), F32),
        pltpu.VMEM((nt, piece, chans), BF16),
        pltpu.VMEM((nt, piece, chans), BF16),
        pltpu.VMEM((nr // 2, piece, chans), F32),
        pltpu.VMEM((2, nt, piece, chans), BF16),
        dma((2,)), dma((fd,)), dma((5,)),
        dma((2, 2)), dma((2, 2)), dma((2,)), dma((2,)), dma((2, 2)), dma((2, 2)),
        dma((1,)), dma((1,)), dma((nr,)), dma((nr,)), dma((nr,)), dma((nr,)),
        dma((1,)), dma((1,)), dma((nt,)), dma((nt,)), dma((nr // 2,)), dma((nr // 2,)),
        dma((nt,)), dma((nt,)), dma((1,)), dma((1,)),
    ]
    factor = 1.0 / math.sqrt(fd * rd * width * nt * nr)
    results = pl.pallas_call(
        functools.partial(kernel, nt, nr, factor),
        out_shape=(
            jax.ShapeDtypeStruct(video.shape, BF16),
            jax.ShapeDtypeStruct((3, 3, chans, chans), F32),
            jax.ShapeDtypeStruct((3, chans, chans), F32),
            jax.ShapeDtypeStruct((fd // nr, nr, width // PATCH), F32),
        ),
        in_specs=[hbm] * 7,
        out_specs=(pl.BlockSpec(memory_space=pl.ANY), vmem, vmem, vmem),
        scratch_shapes=scratch,
        compiler_params=pltpu.CompilerParams(
            collective_id=0, has_side_effects=True, vmem_limit_bytes=60 * 1024 * 1024
        ),
        cost_estimate=pl.CostEstimate(
            flops=2 * fd * rd * width * chans * chans * 36,
            bytes_accessed=3 * fd * rd * width * chans * 2,
            transcendentals=fd * rd * width * chans,
        ),
        name="block_step",
    )(video, w_space, w_time, w_pixel, w_patch, w_logit.reshape(2, chans), grad_out)
    anywhere = pl.BlockSpec(memory_space=pl.ANY)
    return pl.pallas_call(
        hand_over,
        out_shape=[jax.ShapeDtypeStruct(x.shape, x.dtype) for x in results],
        in_specs=[anywhere] * 4,
        out_specs=[anywhere] * 4,
        scratch_shapes=[pltpu.VMEM(x.shape, x.dtype) for x in results] + [dma((2, fd + 3))],
        name="hand_over",
    )(*results)


def solution(mesh):
    in_specs = (P("tm", "rows", None, None), P(), P(), P(), P(), P(), P("tm", "rows", None, None))
    out_specs = (P("tm", "rows", None, None), P(), P(), P(("tm", "rows"), None, None))
    return jax.shard_map(shards, mesh=mesh, in_specs=in_specs, out_specs=out_specs, check_vma=False)
```
